128 devices in a mesh: layer: 8 (over x, z_lo), dp: 16 (over z_hi, y, core).
Axes of the slice: x: 4, y: 4, z: 4 (z_hi: 2, z_lo: 2; z = z_hi * 2 + z_lo), core: 2. Of those that a mesh axis runs over, the one named last changes fastest.
Arguments:
- coarse_guess: bfloat16 [8, 2048, 1024], P('layer', 'dp'), may hold values from -6 to 6
- adjoint_guess: bfloat16 [8, 2048, 1024], P('layer', 'dp'), may hold values from -6 to 6
- w_first: bfloat16 [16, 1024, 2048], P('layer'), may hold values from -0.1875 to 0.1875
- w_second: bfloat16 [16, 2048, 1024], P('layer'), may hold values from -0.125 to 0.125
Outputs:
- new_states: bfloat16 [8, 2048, 1024], P('layer', 'dp')
- new_adjoint: bfloat16 [8, 2048, 1024], P('layer', 'dp')
- grad_first: bfloat16 [16, 1024, 2048], P('layer', 'dp')
- grad_second: bfloat16 [16, 2048, 1024], P('layer', 'dp')
The draws below stay inside these ranges and needn't reach their ends.
All inputs are finite; a program needn't handle non-finite values.
Results may differ from the reference program's by a relative error of at most 0.025.
Values may be sent and summed in bfloat16 or wider, within the bound.
A program may use at most 128 MiB of HBM per device.

```python
import jax
import jax.numpy as jnp
from jax import lax

D = 1024
HIDDEN_SIZE = 2048
LAYERS_DEV = 2
LAYERS = 16
ROWS = 2048
N_LAYER = 8
N_DP = 16


def steps_of(own_key, extent, shards, low, largest):
    def one(position, shards_of):
        steps = jax.random.uniform(jax.random.fold_in(jax.random.fold_in(own_key, 6), position), (shards_of,), jnp.float32, low / len(shards), largest / len(shards))
        return jnp.repeat(jnp.exp(steps), extent[position] // shards_of).reshape((-1,) + (1,) * (len(extent) - position - 1))

    factor_of = one(*shards[0])
    for cut in shards[1:]:
        factor_of = factor_of * one(*cut)
    return factor_of


def scatter_about(own_key, extent, scale, limit, shards=(), held_as=jnp.bfloat16):
    array = scale * jax.random.normal(own_key, extent, jnp.float32)
    if shards:
        array = array * steps_of(own_key, extent, shards, -0.22, 0.18)
    return jnp.clip(array, -limit, limit).astype(held_as)


def setup_inputs(seed: int = 0) -> dict:
    key_of = jax.random.split(jax.random.key(seed), 5)
    return {
        "coarse_guess": scatter_about(key_of[0], (N_LAYER, ROWS, D), 1.0, 6.0, ((0, 8), (1, 16))),
        "adjoint_guess": scatter_about(key_of[1], (N_LAYER, ROWS, D), 1.0, 6.0, ((0, 8), (1, 16))),
        "w_first": scatter_about(key_of[2], (LAYERS, D, HIDDEN_SIZE), D ** -0.5, 0.1875, ((0, 8),)),
        "w_second": scatter_about(key_of[3], (LAYERS, HIDDEN_SIZE, D), HIDDEN_SIZE ** -0.5, 0.125, ((0, 8),)),
    }


step_size = 0.25


def silu_slope(preact):
    logistic = jax.nn.sigmoid(preact)
    return logistic * (1.0 + preact * (1.0 - logistic))


def layer_parts(current, w_in, w_out):
    preact = jnp.dot(current.astype(jnp.bfloat16), w_in, preferred_element_type=jnp.float32)
    hidden_act = jax.nn.silu(preact).astype(jnp.bfloat16)
    layer_out = jnp.dot(hidden_act, w_out, preferred_element_type=jnp.float32)
    return preact, hidden_act, layer_out


def back_parts(adjoint, preact, w_in, w_out, factor):
    adjoint_low = adjoint.astype(jnp.bfloat16)
    pulled = factor * jnp.dot(adjoint_low, w_out.T, preferred_element_type=jnp.float32)
    dpre_low = (pulled * silu_slope(preact)).astype(jnp.bfloat16)
    lifted = jnp.dot(dpre_low, w_in.T, preferred_element_type=jnp.float32)
    return adjoint_low, dpre_low, lifted


def group_sum(left_rows, right_rows, factor):
    left_groups = left_rows.astype(jnp.float32).reshape(N_DP, -1, left_rows.shape[1])
    right_groups = right_rows.astype(jnp.float32).reshape(N_DP, -1, right_rows.shape[1])
    partial_sums = factor * jnp.einsum("gra,grb->gab", left_groups, right_groups)
    rounded = lax.optimization_barrier(partial_sums.astype(jnp.bfloat16))
    return jnp.sum(rounded.astype(jnp.float32), axis=0).astype(jnp.bfloat16)


def reference(coarse_guess, adjoint_guess, w_first, w_second):
    per_block = LAYERS_DEV
    coarse_step = per_block * step_size
    starts = coarse_guess.astype(jnp.float32)
    guesses = adjoint_guess.astype(jnp.float32)
    entering = starts[0]
    new_states = []
    enterings = []
    backed = []
    grads_in = []
    grads_out = []
    for segment in range(N_LAYER):
        first_layer = segment * per_block
        begin_state = starts[segment]
        layer_out = layer_parts(begin_state, w_first[first_layer], w_second[first_layer])[2]
        coarse_from = begin_state + coarse_step * layer_out
        relaxed = begin_state + step_size * layer_out
        for offset in range(1, per_block):
            relaxed = relaxed + step_size * layer_parts(relaxed, w_first[first_layer + offset], w_second[first_layer + offset])[2]
        preact, hidden_act, layer_out = layer_parts(entering, w_first[first_layer], w_second[first_layer])
        leaving = (relaxed + (entering + coarse_step * layer_out) - coarse_from).astype(jnp.bfloat16)
        new_states.append(leaving)
        inputs = [entering]
        pre_list = [preact]
        act_list = [hidden_act]
        current = entering + step_size * layer_out
        for offset in range(1, per_block):
            preact, hidden_act, layer_out = layer_parts(current, w_first[first_layer + offset], w_second[first_layer + offset])
            inputs.append(current)
            pre_list.append(preact)
            act_list.append(hidden_act)
            current = current + step_size * layer_out
        adjoint = guesses[segment]
        block_in = [None] * per_block
        block_out = [None] * per_block
        for offset in reversed(range(per_block)):
            adjoint_low, dpre_low, lifted = back_parts(adjoint, pre_list[offset], w_first[first_layer + offset], w_second[first_layer + offset], step_size)
            block_out[offset] = group_sum(act_list[offset], adjoint_low, step_size)
            block_in[offset] = group_sum(inputs[offset].astype(jnp.bfloat16), dpre_low, 1.0)
            adjoint = adjoint + lifted
        grads_in = grads_in + block_in
        grads_out = grads_out + block_out
        backed.append(adjoint)
        enterings.append(entering)
        entering = leaving.astype(jnp.float32)
    arriving = guesses[N_LAYER - 1]
    new_adjoint = [None] * N_LAYER
    for segment in reversed(range(N_LAYER)):
        first_layer = segment * per_block
        preact = layer_parts(enterings[segment], w_first[first_layer], w_second[first_layer])[0]
        difference = arriving - guesses[segment]
        lifted = back_parts(difference, preact, w_first[first_layer], w_second[first_layer], coarse_step)[2]
        settled = (backed[segment] + difference + lifted).astype(jnp.bfloat16)
        new_adjoint[segment] = settled
        arriving = settled.astype(jnp.float32)
    return jnp.stack(new_states), jnp.stack(new_adjoint), jnp.stack(grads_in), jnp.stack(grads_out)
```

```python
import functools

import jax
import jax.numpy as jnp
from jax import lax
from jax.experimental import pallas as pl
from jax.experimental.pallas import tpu as pltpu
from jax.sharding import PartitionSpec as P

MESH = pl.DeviceIdType.MESH
f32 = jnp.float32
bf16 = jnp.bfloat16
STEP = 0.25
NC = 4
NT = (((1,), (1,)), ((), ()))
TN = (((0,), (0,)), ((), ()))


def mm(x, w):
    return jnp.dot(x, w, preferred_element_type=f32)


def mm_nt(x, w):
    return lax.dot_general(x, w, NT, preferred_element_type=f32)


def mm_tn(x, w):
    return lax.dot_general(x, w, TN, preferred_element_type=f32)


def slope_of(pre):
    sig = jax.nn.sigmoid(pre)
    return sig * (1.0 + pre * (1.0 - sig))


def kernel(
    g_hbm, a_hbm, w1_hbm, w2_hbm,
    ns_out, na_out, g1_out, g2_out,
    w1, w2, w1t, w2t, g, a,
    vbuf, nbuf, arr, abuf, pre0, work, base, out0, y1,
    act0, act1, s1p, s1c,
    lhs_a, lhs_s, rhs_y, rhs_d, dl,
    core_a, core_s, ring_a, ring_s,
    ld, vs, vr, asn, ar, zs, zr, ds, dr, ys, yr,
):
    rows, width = g.shape
    hidden = w1.shape[2]
    col = width // NC
    half = hidden // 2
    hid = hidden // 4
    p = lax.axis_index("layer")
    dp = lax.axis_index("dp")
    h = dp // 8
    y = (dp // 2) % 4
    c = dp % 2
    y_up, y_dn, y_far = (y + 1) % 4, (y + 3) % 4, (y + 2) % 4
    at_z = (p, (1 - h) * 8 + y * 2 + c)
    at_core = (p, h * 8 + y * 2 + (1 - c))
    at_up = (p, h * 8 + y_up * 2 + c)
    at_dn = (p, h * 8 + y_dn * 2 + c)
    at_next = ((p + 1) % 8, dp)
    at_prev = ((p + 7) % 8, dp)

    barrier = pltpu.get_barrier_semaphore()
    for peer in (at_z, at_core, at_up, at_dn, at_next, at_prev):
        pl.semaphore_signal(barrier, inc=1, device_id=peer, device_id_type=MESH)

    loads = [
        pltpu.make_async_copy(g_hbm.at[0], g, ld.at[0]),
        pltpu.make_async_copy(w1_hbm.at[0], w1.at[0], ld.at[1]),
        pltpu.make_async_copy(w2_hbm.at[0], w2.at[0], ld.at[2]),
        pltpu.make_async_copy(w1_hbm.at[1], w1.at[1], ld.at[3]),
        pltpu.make_async_copy(w2_hbm.at[1], w2.at[1], ld.at[4]),
        pltpu.make_async_copy(a_hbm.at[0], a, ld.at[5]),
    ]
    for load in loads:
        load.start()

    def remote(src, dst, ss, rs, dev):
        return pltpu.make_async_remote_copy(
            src_ref=src, dst_ref=dst, send_sem=ss, recv_sem=rs, device_id=dev, device_id_type=MESH
        )

    v_send = [remote(nbuf.at[k], vbuf.at[k], vs.at[k], vr.at[k], at_next) for k in range(NC)]
    a_send = [remote(abuf.at[k], arr.at[k], asn.at[k], ar.at[k], at_prev) for k in range(NC)]

    def hs(j):
        return pl.ds(j * hid, hid)

    def cs(n):
        return pl.ds(n * col, col)

    def second(act, layer, n):
        return mm(act[0], w2[layer, pl.ds(0, half), cs(n)]) + mm(
            act[1], w2[layer, pl.ds(half, half), cs(n)]
        )

    def put_act(act, j, value):
        act[j // 2, :, pl.ds((j % 2) * hid, hid)] = value

    loads[0].wait()
    loads[1].wait()
    for j in range(4):
        pre = mm(g[...], w1[0, :, hs(j)])
        pre0[:, hs(j)] = pre
        put_act(act0, j, (pre * jax.nn.sigmoid(pre)).astype(bf16))
    loads[2].wait()
    for n in range(NC):
        out = second(act0, 0, n)
        out0[:, cs(n)] = out
        s1p[:, cs(n)] = (g[:, cs(n)].astype(f32) + STEP * out).astype(bf16)
    loads[3].wait()
    for j in range(4):
        pre = mm(s1p[...], w1[1, :, hs(j)])
        put_act(act1, j, (pre * jax.nn.sigmoid(pre)).astype(bf16))
    loads[4].wait()
    pl.semaphore_wait(barrier, 6)
    for n in range(NC):
        begin = g[:, cs(n)].astype(f32)
        out = out0[:, cs(n)]
        relaxed = begin + STEP * out + STEP * second(act1, 1, n)
        base_n = relaxed - (begin + 2 * STEP * out)
        base[:, cs(n)] = base_n

        @pl.when(p == 0)
        def _():
            vbuf[n] = g[:, cs(n)]
            new = (base_n + (begin + 2 * STEP * out)).astype(bf16)
            nbuf[n] = new
            v_send[n].start()
            ns_out[0, :, cs(n)] = new

    loads[5].wait()

    def prepare():
        for j in range(4):
            work[:, hs(j)] = STEP * mm_nt(a[...], w2[1, hs(j), :])

    def transpose():
        for j in range(4):
            for n in range(NC):
                w2t[cs(n), hs(j)] = w2[0, hs(j), cs(n)].T
                w1t[hs(j), cs(n)] = w1[0, cs(n), hs(j)].T

    @pl.when(p > 0)
    def _():
        prepare()

    @pl.when(p > 1)
    def _():
        transpose()

    @pl.when(p > 0)
    def _():
        for k in range(NC):
            v_send[k].wait_recv()
            for j in range(4):
                pre = mm(vbuf[k], w1[0, cs(k), hs(j)])
                if k:
                    pre = pre + pre0[:, hs(j)]
                pre0[:, hs(j)] = pre
                if k == NC - 1:
                    put_act(act0, j, (pre * jax.nn.sigmoid(pre)).astype(bf16))
        for n in range(NC):
            out = second(act0, 0, n)
            out0[:, cs(n)] = out
            new = (base[:, cs(n)] + (vbuf[n].astype(f32) + 2 * STEP * out)).astype(bf16)
            nbuf[n] = new

            @pl.when(p < 7)
            def _():
                v_send[n].start()

            ns_out[0, :, cs(n)] = new

    @pl.when(p == 0)
    def _():
        prepare()

    @pl.when(p < 2)
    def _():
        transpose()

    z_copies = [
        remote(act1.at[1 - h], lhs_a.at[0, pl.ds(rows, rows)], zs.at[0], zr.at[0], at_z),
        remote(a, rhs_y.at[0, pl.ds(rows, rows)], zs.at[1], zr.at[1], at_z),
        remote(s1c.at[pl.ds(2 * (1 - h), 2)], lhs_s.at[0, :, pl.ds(rows, rows)], zs.at[2], zr.at[2], at_z),
        remote(rhs_d.at[0, pl.ds(0, rows)], rhs_d.at[0, pl.ds(rows, rows)], zs.at[3], zr.at[3], at_z),
        remote(act0.at[1 - h], lhs_a.at[1, pl.ds(rows, rows)], zs.at[4], zr.at[4], at_z),
        remote(rhs_y.at[1, pl.ds(0, rows)], rhs_y.at[1, pl.ds(rows, rows)], zs.at[5], zr.at[5], at_z),
        remote(vbuf.at[pl.ds(2 * (1 - h), 2)], lhs_s.at[1, :, pl.ds(rows, rows)], zs.at[6], zr.at[6], at_z),
        remote(rhs_d.at[1, pl.ds(0, rows)], rhs_d.at[1, pl.ds(rows, rows)], zs.at[7], zr.at[7], at_z),
    ]
    z_copies[1].start()
    z_copies[6].start()
    z_copies[4].start()
    for n in range(NC):
        state = (vbuf[n].astype(f32) + STEP * out0[:, cs(n)]).astype(bf16)
        s1p[:, cs(n)] = state
        s1c[n] = state
    z_copies[2].start()
    for j in range(4):
        pre = mm(s1p[...], w1[1, :, hs(j)])
        sig = jax.nn.sigmoid(pre)
        put_act(act1, j, (pre * sig).astype(bf16))
        rhs_d[0, pl.ds(0, rows), hs(j)] = (
            work[:, hs(j)] * (sig * (1.0 + pre * (1.0 - sig)))
        ).astype(bf16)
        pre0[:, hs(j)] = slope_of(pre0[:, hs(j)])
    z_copies[0].start()
    z_copies[3].start()
    for n in range(NC):
        y1_n = a[:, cs(n)].astype(f32) + mm_nt(rhs_d[0, pl.ds(0, rows), :], w1[1, cs(n), :])
        y1[:, cs(n)] = y1_n
        rhs_y[1, pl.ds(0, rows), cs(n)] = y1_n.astype(bf16)
    z_copies[5].start()
    for j in range(4):
        pulled = STEP * mm(rhs_y[1, pl.ds(0, rows), :], w2t[:, hs(j)])
        rhs_d[1, pl.ds(0, rows), hs(j)] = (pulled * pre0[:, hs(j)]).astype(bf16)
    z_copies[7].start()
    for n in range(NC):
        y1[:, cs(n)] = y1[:, cs(n)] + mm(rhs_d[1, pl.ds(0, rows), :], w1t[:, cs(n)])

    @pl.when(p == 7)
    def _():
        for k in range(NC):
            arr[k] = a[:, cs(k)]

    def settle():
        for k in range(NC):
            @pl.when(p < 7)
            def _():
                a_send[k].wait_recv()

            diff = (arr[k].astype(f32) - a[:, cs(k)].astype(f32)).astype(bf16)
            for j in range(4):
                pulled = mm(diff, w2t[cs(k), hs(j)])
                if k:
                    pulled = pulled + work[:, hs(j)]
                if k < NC - 1:
                    work[:, hs(j)] = pulled
                else:
                    dl[:, hs(j)] = (2 * STEP * pulled * pre0[:, hs(j)]).astype(bf16)
        for n in range(NC):
            lifted = mm(dl[...], w1t[:, cs(n)])
            diff = arr[n].astype(f32) - a[:, cs(n)].astype(f32)
            new = (y1[:, cs(n)] + diff + lifted).astype(bf16)
            abuf[n] = new

            @pl.when(p > 0)
            def _():
                a_send[n].start()

            na_out[0, :, cs(n)] = new

    def part(u):
        i = u // 2
        if u % 2 == 0:
            size = hidden // 16
            store, start = w2, i * 8 * size
            got, ring, out = core_a.at[i], ring_a.at[i], g2_out
        else:
            size = width // 16
            store, start = w1, i * 8 * size
            got, ring, out = core_s.at[i], ring_s.at[i], g1_out

        def block(cc, yy, lo=0, n=size):
            return (1, pl.ds(start + (cc * 4 + yy) * size + lo, n))

        return size, store, block, got, ring, out

    def core_copy(u):
        size, store, block, got, ring, out = part(u)
        return remote(store.at[block(1 - c, 0, 0, 4 * size)], got, ds.at[u], dr.at[u], at_core)

    def ring_copies(u):
        size, store, block, got, ring, out = part(u)
        hf = size // 2
        plan = [
            (block(c, y_far, 0, hf), (0, 0), at_up),
            (block(c, y_far, hf, hf), (0, 1), at_dn),
            (block(c, y_up, hf, hf), (1, 1), at_up),
            (block(c, y_dn, 0, hf), (2, 0), at_dn),
            (block(c, y_up, 0, hf), (1, 0), at_up),
            (block(c, y_dn, hf, hf), (2, 1), at_dn),
        ]
        return [
            remote(store.at[src], ring.at[dst], ys.at[u * 6 + m], yr.at[u * 6 + m], dev)
            for m, (src, dst, dev) in enumerate(plan)
        ]

    def product(u):
        size, store, block, got, ring, out = part(u)
        i = u // 2
        if u == 0:
            rhs_y[0, pl.ds(0, rows), :] = a[...]
        if u % 2 == 0:
            lhs_a[i, pl.ds(0, rows), :] = (act1 if i == 0 else act0)[h]
        else:
            for kk in range(2):
                lhs_s[i, kk, pl.ds(0, rows), :] = (s1c if i == 0 else vbuf)[2 * h + kk]
        z_copies[2 * u].wait_recv()
        z_copies[2 * u + 1].wait_recv()
        for yy in range(4):
            if u % 2 == 0:
                res = STEP * mm_tn(lhs_a[i, :, pl.ds(yy * 2 * size, 2 * size)], rhs_y[i])
            else:
                res = mm_tn(lhs_s[i, yy // 2, :, pl.ds((yy % 2) * 2 * size, 2 * size)], rhs_d[i])
            res = res.astype(bf16)
            for cc in range(2):
                store[block(cc, yy)] = res[cc * size:(cc + 1) * size]
        core_copy(u).start()

    def pair_sum(u):
        size, store, block, got, ring, out = part(u)
        core_copy(u).wait_recv()
        copies = ring_copies(u)

        def add(yy):
            at = pl.ds(pl.multiple_of(yy * size, size), size)
            store[block(c, yy)] = (store[block(c, yy)].astype(f32) + got[at].astype(f32)).astype(bf16)

        add(y_far)
        copies[0].start()
        copies[1].start()
        add(y_up)
        copies[2].start()
        add(y_dn)
        copies[3].start()
        add(y)

    def pass_on(u):
        size, store, block, got, ring, out = part(u)
        hf = size // 2
        copies = ring_copies(u)
        for m, yy, lo in ((0, y_up, 0), (1, y_dn, hf)):
            copies[m].wait_recv()
            at = block(c, yy, lo, hf)
            store[at] = (store[at].astype(f32) + ring[0, m].astype(f32)).astype(bf16)
            copies[4 + m].start()

    def finish(u):
        size, store, block, got, ring, out = part(u)
        hf = size // 2
        copies = ring_copies(u)
        for m in (2, 3, 4, 5):
            copies[m].wait_recv()
        for m in range(2):
            total = (
                store[block(c, y, m * hf, hf)].astype(f32)
                + ring[1, m].astype(f32)
                + ring[2, m].astype(f32)
            )
            out[1 - u // 2, pl.ds(m * hf, hf), :] = total.astype(bf16)

    order = [
        (7, 7),
        (product, 0), (product, 1), (pair_sum, 0), (6, 6),
        (product, 2), (pair_sum, 1), (pass_on, 0),
        (product, 3), (5, 5), (pair_sum, 2), (pass_on, 1), (finish, 0),
        (pair_sum, 3), (3, 4), (pass_on, 2), (finish, 1), (pass_on, 3), (finish, 2), (finish, 3),
        (0, 2),
    ]
    for what, u in order:
        if callable(what):
            what(u)
        else:
            @pl.when(jnp.logical_and(p >= what, p <= u))
            def _():
                settle()

    for copy in z_copies:
        copy.wait_send()
    for u in range(4):
        core_copy(u).wait_send()
        for copy in ring_copies(u):
            copy.wait_send()

    @pl.when(p < 7)
    def _():
        for copy in v_send:
            copy.wait_send()

    @pl.when(p > 0)
    def _():
        for copy in a_send:
            copy.wait_send()


def body(coarse_guess, adjoint_guess, w_first, w_second):
    layers, width, hidden = w_first.shape
    rows = coarse_guess.shape[1]
    col = width // NC
    vmem = pltpu.VMEM
    dma = pltpu.SemaphoreType.DMA
    hw, sw = hidden // 16, width // 16
    return pl.pallas_call(
        kernel,
        out_shape=(
            jax.ShapeDtypeStruct((1, rows, width), bf16),
            jax.ShapeDtypeStruct((1, rows, width), bf16),
            jax.ShapeDtypeStruct((layers, sw, hidden), bf16),
            jax.ShapeDtypeStruct((layers, hw, width), bf16),
        ),
        in_specs=[pl.BlockSpec(memory_space=pl.ANY)] * 4,
        out_specs=[pl.BlockSpec(memory_space=pltpu.VMEM)] * 4,
        scratch_shapes=[
            vmem((layers, width, hidden), bf16),
            vmem((layers, hidden, width), bf16),
            vmem((hidden, width), bf16),
            vmem((width, hidden), bf16),
            vmem((rows, width), bf16),
            vmem((rows, width), bf16),
            vmem((NC, rows, col), bf16),
            vmem((NC, rows, col), bf16),
            vmem((NC, rows, col), bf16),
            vmem((NC, rows, col), bf16),
            vmem((rows, hidden), f32),
            vmem((rows, hidden), f32),
            vmem((rows, width), f32),
            vmem((rows, width), f32),
            vmem((rows, width), f32),
            vmem((2, rows, hidden // 2), bf16),
            vmem((2, rows, hidden // 2), bf16),
            vmem((rows, width), bf16),
            vmem((NC, rows, col), bf16),
            vmem((2, 2 * rows, hidden // 2), bf16),
            vmem((2, 2, 2 * rows, col), bf16),
            vmem((2, 2 * rows, width), bf16),
            vmem((2, 2 * rows, hidden), bf16),
            vmem((rows, hidden), bf16),
            vmem((2, 4 * hw, width), bf16),
            vmem((2, 4 * sw, hidden), bf16),
            vmem((2, 3, 2, hw // 2, width), bf16),
            vmem((2, 3, 2, sw // 2, hidden), bf16),
            dma((6,)),
            dma((NC,)),
            dma((NC,)),
            dma((NC,)),
            dma((NC,)),
            dma((8,)),
            dma((8,)),
            dma((4,)),
            dma((4,)),
            dma((24,)),
            dma((24,)),
        ],
        compiler_params=pltpu.CompilerParams(
            collective_id=0, has_side_effects=True, vmem_limit_bytes=60 << 20
        ),
        name="mgrit",
    )(coarse_guess, adjoint_guess, w_first, w_second)


def solution(mesh):
    in_specs = (
        P("layer", "dp", None),
        P("layer", "dp", None),
        P("layer", None, None),
        P("layer", None, None),
    )
    out_specs = (
        P("layer", "dp", None),
        P("layer", "dp", None),
        P("layer", "dp", None),
        P("layer", "dp", None),
    )
    return jax.shard_map(body, mesh=mesh, in_specs=in_specs, out_specs=out_specs, check_vma=False)
```

```python
import functools

import jax
import jax.numpy as jnp
from jax import lax
from jax.experimental import pallas as pl
from jax.experimental.pallas import tpu as pltpu
from jax.sharding import PartitionSpec as P

MESH = pl.DeviceIdType.MESH
f32 = jnp.float32
bf16 = jnp.bfloat16
STEP = 0.25
NC = 4
NT = (((1,), (1,)), ((), ()))
TN = (((0,), (0,)), ((), ()))


def mm(x, w):
    return jnp.dot(x, w, preferred_element_type=f32)


def mm_nt(x, w):
    return lax.dot_general(x, w, NT, preferred_element_type=f32)


def mm_tn(x, w):
    return lax.dot_general(x, w, TN, preferred_element_type=f32)


def slope_of(pre):
    sig = jax.nn.sigmoid(pre)
    return sig * (1.0 + pre * (1.0 - sig))


def kernel(
    g_hbm, a_hbm, w1_hbm, w2_hbm,
    ns_out, na_out, g1_out, g2_out,
    w1, w2, w1t, w2t, g, a,
    vbuf, nbuf, arr, abuf, pre0, work, base, out0, y1,
    act0, act1, s1p, s1c,
    lhs_a, rhs_y, lhs_s, rhs_d, dpre, dl, acc, w1t1, home_s, home_a, part_z, got_z,
    core_a, core_s, ring_a, ring_s,
    ld, vs, vr, asn, ar, zs, zr, ds, dr, ys, yr, hs_s, hs_r, fs, fr,
):
    rows, width = g.shape
    hidden = w1.shape[2]
    col = width // NC
    half = hidden // 2
    hid = hidden // 4
    p = lax.axis_index("layer")
    dp = lax.axis_index("dp")
    h = dp // 8
    y = (dp // 2) % 4
    c = dp % 2
    y_up, y_dn, y_far = (y + 1) % 4, (y + 3) % 4, (y + 2) % 4
    at_z = (p, (1 - h) * 8 + y * 2 + c)
    at_core = (p, h * 8 + y * 2 + (1 - c))
    at_up = (p, h * 8 + y_up * 2 + c)
    at_dn = (p, h * 8 + y_dn * 2 + c)
    other = (1 - h) * 8 + y * 2 + c
    zhop = 1 - p % 2
    at_next, at_prev = (), ()
    for m in range(2):
        turn_next = zhop * m + (1 - zhop) * c
        turn_prev = (1 - zhop) * m + zhop * c
        at_next += (((p + 1) % 8, dp * (1 - turn_next) + other * turn_next),)
        at_prev += (((p + 7) % 8, dp * (1 - turn_prev) + other * turn_prev),)
    away = [(m * ((p + 1) // 2) + c * (p // 2)) % 2 == 1 for m in range(2)]
    rh = rows // 2
    halves = (pl.ds(0, rh), pl.ds(rh, rh))

    barrier = pltpu.get_barrier_semaphore()
    for peer in (at_z, at_core, at_up, at_dn, *at_next, *at_prev):
        pl.semaphore_signal(barrier, inc=1, device_id=peer, device_id_type=MESH)

    loads = []
    for layer in range(2):
        for store, src in ((w1, w1_hbm), (w2, w2_hbm)):
            size = store.shape[2] // 2
            for m in range(2):
                at = (layer, slice(None), pl.ds(m * size, size))
                loads.append(pltpu.make_async_copy(src.at[at], store.at[at], ld.at[len(loads)]))
    local = [
        pltpu.make_async_copy(src.at[0, halves[m]], dst.at[halves[m]], ld.at[8 + 2 * i + m])
        for i, (src, dst) in enumerate(((g_hbm, g), (a_hbm, a)))
        for m in range(2)
    ]

    def guess(what, i, remote_copies):
        for m in range(2):
            @pl.when(away[m])
            def _():
                if what == "remote":
                    remote_copies[2 * i + m].start()
                elif what == "wait":
                    remote_copies[2 * i + m].wait_recv()

            @pl.when(jnp.logical_not(away[m]))
            def _():
                if what == "local":
                    local[2 * i + m].start()
                elif what == "wait":
                    local[2 * i + m].wait()

    def remote(src, dst, ss, rs, dev):
        return pltpu.make_async_remote_copy(
            src_ref=src, dst_ref=dst, send_sem=ss, recv_sem=rs, device_id=dev, device_id_type=MESH
        )

    def hop(src, dst, ss, rs, peers):
        return [
            [
                remote(src.at[k, at], dst.at[k, at], ss.at[2 * k + m], rs.at[2 * k + m], peers[m])
                for m, at in enumerate(halves)
            ]
            for k in range(NC)
        ]

    v_send = hop(nbuf, vbuf, vs, vr, at_next)
    a_send = hop(abuf, arr, asn, ar, at_prev)
    swap = [
        remote(src.at[0, halves[m]], dst.at[halves[m]], hs_s.at[2 * i + m], hs_r.at[2 * i + m], at_z)
        for i, (src, dst) in enumerate(((g_hbm, g), (a_hbm, a)))
        for m in range(2)
    ]
    back = [
        [
            [
                remote(
                    src.at[k, halves[m]], dst.at[k, halves[m]],
                    hs_s.at[4 + (i * NC + k) * 2 + m], hs_r.at[4 + (i * NC + k) * 2 + m], at_z,
                )
                for m in range(2)
            ]
            for k in range(NC)
        ]
        for i, (src, dst) in enumerate(((nbuf, home_s), (abuf, home_a)))
    ]

    def send_back(copies):
        for m in range(2):
            @pl.when(away[m])
            def _():
                copies[m].start()

    def hs(j):
        return pl.ds(j * hid, hid)

    def cs(n):
        return pl.ds(n * col, col)

    def second(act, layer, n):
        return mm(act[0], w2[layer, pl.ds(0, half), cs(n)]) + mm(
            act[1], w2[layer, pl.ds(half, half), cs(n)]
        )

    def put_act(act, j, value):
        act[j // 2, :, pl.ds((j % 2) * hid, hid)] = value

    guess("local", 0, swap)
    for load in loads:
        load.start()
    guess("local", 1, swap)

    @pl.when(p > 0)
    def _():
        pl.semaphore_wait(barrier, 8)

    guess("remote", 0, swap)
    guess("remote", 1, swap)
    guess("wait", 0, swap)
    for j in range(4):
        if j % 2 == 0:
            loads[j // 2].wait()
        pre = mm(g[...], w1[0, :, hs(j)])
        pre0[:, hs(j)] = pre
        put_act(act0, j, (pre * jax.nn.sigmoid(pre)).astype(bf16))
    for n in range(NC):
        if n % 2 == 0:
            loads[2 + n // 2].wait()
        out = second(act0, 0, n)
        out0[:, cs(n)] = out
        s1p[:, cs(n)] = (g[:, cs(n)].astype(f32) + STEP * out).astype(bf16)
    for j in range(4):
        if j % 2 == 0:
            loads[4 + j // 2].wait()
        pre = mm(s1p[...], w1[1, :, hs(j)])
        put_act(act1, j, (pre * jax.nn.sigmoid(pre)).astype(bf16))

    @pl.when(p == 0)
    def _():
        pl.semaphore_wait(barrier, 8)

    for n in range(NC):
        if n % 2 == 0:
            loads[6 + n // 2].wait()
        begin = g[:, cs(n)].astype(f32)
        out = out0[:, cs(n)]
        relaxed = begin + STEP * out + STEP * second(act1, 1, n)
        base_n = relaxed - (begin + 2 * STEP * out)
        base[:, cs(n)] = base_n

        @pl.when(p == 0)
        def _():
            vbuf[n] = g[:, cs(n)]
            nbuf[n] = (base_n + (begin + 2 * STEP * out)).astype(bf16)
            for copy in v_send[n]:
                copy.start()

    guess("wait", 1, swap)
    early = remote(a, rhs_y.at[0, pl.ds(rows, rows)], zs.at[0], zr.at[0], at_z)

    @pl.when(p > 1)
    def _():
        early.start()

    def prepare():
        for j in range(4):
            work[:, hs(j)] = STEP * mm_nt(a[...], w2[1, hs(j), :])

    def transpose():
        for j in range(4):
            for n in range(NC):
                w2t[cs(n), hs(j)] = w2[0, hs(j), cs(n)].T
                w1t[hs(j), cs(n)] = w1[0, cs(n), hs(j)].T
                w1t1[hs(j), cs(n)] = w1[1, cs(n), hs(j)].T

    @pl.when(p > 0)
    def _():
        prepare()

    def pull(k, save=True):
        diff = (arr[k].astype(f32) - a[:, cs(k)].astype(f32)).astype(bf16)
        for j in range(4):
            pulled = mm(diff, w2t[cs(k), hs(j)])
            if k:
                pulled = pulled + acc[:, hs(j)]
            if save:
                acc[:, hs(j)] = pulled
            else:
                dl[:, hs(j)] = (2 * STEP * pulled * pre0[:, hs(j)]).astype(bf16)

    @pl.when(p > 1)
    def _():
        transpose()

    @pl.when(p == 7)
    def _():
        for k in range(NC):
            arr[k] = a[:, cs(k)]
        for k in range(NC):
            pull(k)

    @pl.when(p > 0)
    def _():
        for k in range(NC):
            for copy in v_send[k]:
                copy.wait_recv()
            for j in range(4):
                pre = mm(vbuf[k], w1[0, cs(k), hs(j)])
                if k:
                    pre = pre + pre0[:, hs(j)]
                pre0[:, hs(j)] = pre
                if k == NC - 1:
                    put_act(act0, j, (pre * jax.nn.sigmoid(pre)).astype(bf16))

    def advance(sending):
        for n in range(NC):
            out = second(act0, 0, n)
            out0[:, cs(n)] = out
            new = (base[:, cs(n)] + (vbuf[n].astype(f32) + 2 * STEP * out)).astype(bf16)
            nbuf[n] = new
            if sending:
                for copy in v_send[n]:
                    copy.start()

    @pl.when(jnp.logical_and(p > 0, p < 7))
    def _():
        advance(True)

    @pl.when(p == 7)
    def _():
        advance(False)

    @pl.when(p == 0)
    def _():
        prepare()

    @pl.when(p < 2)
    def _():
        transpose()

    for n in range(NC):
        ns_out[0, :, cs(n)] = nbuf[n]

    z_copies = [
        early,
        remote(act1.at[1 - h], lhs_a.at[0, pl.ds(rows, rows)], zs.at[1], zr.at[1], at_z),
        remote(act0.at[1 - h], lhs_a.at[1, pl.ds(rows, rows)], zs.at[2], zr.at[2], at_z),
        remote(rhs_y.at[1, pl.ds(0, rows)], rhs_y.at[1, pl.ds(rows, rows)], zs.at[3], zr.at[3], at_z),
        remote(vbuf.at[pl.ds(2 * (1 - h), 2)], lhs_s.at[:, pl.ds(rows, rows)], zs.at[4], zr.at[4], at_z),
        remote(dpre.at[1], rhs_d.at[pl.ds(rows, rows)], zs.at[5], zr.at[5], at_z),
    ]
    @pl.when(p == 7)
    def _():
        z_copies[2].start()

    for n in range(NC):
        state = (vbuf[n].astype(f32) + STEP * out0[:, cs(n)]).astype(bf16)
        s1p[:, cs(n)] = state
        s1c[n] = state
    for j in range(4):
        pre = mm(s1p[...], w1[1, :, hs(j)])
        sig = jax.nn.sigmoid(pre)
        put_act(act1, j, (pre * sig).astype(bf16))
        dpre[0, :, hs(j)] = (
            work[:, hs(j)] * (sig * (1.0 + pre * (1.0 - sig)))
        ).astype(bf16)
        pre0[:, hs(j)] = slope_of(pre0[:, hs(j)])
    for n in range(NC):
        y1_n = a[:, cs(n)].astype(f32) + mm(dpre[0], w1t1[:, cs(n)])
        y1[:, cs(n)] = y1_n
        rhs_y[1, pl.ds(0, rows), cs(n)] = y1_n.astype(bf16)
    for j in range(4):
        pulled = STEP * mm(rhs_y[1, pl.ds(0, rows), :], w2t[:, hs(j)])
        dpre[1, :, hs(j)] = (pulled * pre0[:, hs(j)]).astype(bf16)
    for n in range(NC):
        y1[:, cs(n)] = y1[:, cs(n)] + mm(dpre[1], w1t[:, cs(n)])

    def settle(end, sending=True):
        if end:
            for j in range(4):
                dl[:, hs(j)] = (2 * STEP * acc[:, hs(j)] * pre0[:, hs(j)]).astype(bf16)
        else:
            for k in range(NC):
                for copy in a_send[k]:
                    copy.wait_recv()
                pull(k, k < NC - 1)
        for n in range(NC):
            lifted = mm(dl[...], w1t[:, cs(n)])
            diff = arr[n].astype(f32) - a[:, cs(n)].astype(f32)
            abuf[n] = (y1[:, cs(n)] + diff + lifted).astype(bf16)
            if sending:
                for copy in a_send[n]:
                    copy.start()
        for n in range(NC):
            na_out[0, :, cs(n)] = abuf[n]

    def part(u):
        i = min(u // 2, 1)
        size, start = 128, 0
        if u == 4:
            size = 64
            store, got = w1.at[0], core_s.at[1, pl.ds(0, 4 * size)]
            ring = [[ring_s.at[1, n, m, pl.ds(0, size // 2)] for m in range(2)] for n in range(3)]
        elif u % 2 == 0:
            start = i * 8 * size
            store, got = w2.at[1], core_a.at[i]
            ring = [[ring_a.at[i, n, m] for m in range(2)] for n in range(3)]
        else:
            store, got = w1.at[1 - i], core_s.at[i]
            ring = [[ring_s.at[i, n, m] for m in range(2)] for n in range(3)]

        def block(cc, yy, lo=0, n=size):
            return pl.ds(pl.multiple_of(start + (cc * 4 + yy) * size + lo, size // 2), n)

        return size, store, block, got, ring

    def core_copy(u):
        size, store, block, got, ring = part(u)
        return remote(store.at[block(1 - c, 0, 0, 4 * size)], got, ds.at[min(u, 3)], dr.at[min(u, 3)], at_core)

    def ring_copies(u):
        size, store, block, got, ring = part(u)
        hf = size // 2
        plan = [
            (block(c, y_far, 0, hf), (0, 0), at_up),
            (block(c, y_far, hf, hf), (0, 1), at_dn),
            (block(c, y_up, hf, hf), (1, 1), at_up),
            (block(c, y_dn, 0, hf), (2, 0), at_dn),
            (block(c, y_up, 0, hf), (1, 0), at_up),
            (block(c, y_dn, hf, hf), (2, 1), at_dn),
        ]
        return [
            remote(store.at[src], ring[dst[0]][dst[1]], ys.at[min(u, 3) * 6 + m], yr.at[min(u, 3) * 6 + m], dev)
            for m, (src, dst, dev) in enumerate(plan)
        ]

    def last_copy(u):
        i = u // 2
        return remote(part_z.at[i, 1 - h], got_z.at[i], fs.at[i], fr.at[i], at_z)

    def product(u):
        size, store, block, got, ring = part(u)
        i = u // 2
        if u == 4:
            rhs_d[pl.ds(0, rows), :] = dpre[1]
            for kk in range(2):
                lhs_s[kk, pl.ds(0, rows), :] = vbuf[2 * h + kk]
            for yy in range(4):
                lhs = lhs_s[yy // 2, :, pl.ds((yy % 2) * 2 * size, 2 * size)]
                for piece in range(2):
                    at = pl.ds(piece * half, half)
                    res = mm_tn(lhs, rhs_d[:, at]).astype(bf16)
                    for cc in range(2):
                        store[block(cc, yy), at] = res[cc * size:(cc + 1) * size]
        elif u % 2 == 0:
            if i == 0:
                rhs_y[0, pl.ds(0, rows), :] = a[...]
            lhs_a[i, pl.ds(0, rows), :] = (act1 if i == 0 else act0)[h]
            for yy in range(4):
                res = STEP * mm_tn(lhs_a[i, :, pl.ds(yy * 2 * size, 2 * size)], rhs_y[i])
                res = res.astype(bf16)
                for cc in range(2):
                    store[block(cc, yy)] = res[cc * size:(cc + 1) * size]
        else:
            hf = size // 2
            for kk in range(4):
                lhs = (s1c if i == 0 else vbuf)[kk]
                for piece in range(2):
                    at = pl.ds(piece * half, half)
                    res = mm_tn(lhs, dpre[i, :, at]).astype(bf16)
                    for m in range(4):
                        rows_at = block(m % 2, (kk % 2) * 2 + m // 2, (kk // 2) * hf, hf)
                        store[rows_at, at] = res[m * hf:(m + 1) * hf]
        core_copy(u).start()

    def pair_sum(u):
        size, store, block, got, ring = part(u)
        core_copy(u).wait_recv()
        copies = ring_copies(u)

        def add(yy):
            at = pl.ds(pl.multiple_of(yy * size, size), size)
            store[block(c, yy)] = (store[block(c, yy)].astype(f32) + got[at].astype(f32)).astype(bf16)

        add(y_far)
        copies[0].start()
        copies[1].start()
        add(y_up)
        copies[2].start()
        add(y_dn)
        copies[3].start()
        add(y)

    def pass_on(u):
        size, store, block, got, ring = part(u)
        hf = size // 2
        copies = ring_copies(u)
        for m, yy, lo in ((0, y_up, 0), (1, y_dn, hf)):
            copies[m].wait_recv()
            at = block(c, yy, lo, hf)
            store[at] = (store[at].astype(f32) + ring[0][m][...].astype(f32)).astype(bf16)
            copies[4 + m].start()

    def finish(u):
        size, store, block, got, ring = part(u)
        hf = size // 2
        i = u // 2
        copies = ring_copies(u)
        for m in (2, 3, 4, 5):
            copies[m].wait_recv()
        for m in range(2):
            total = (
                store[block(c, y, m * hf, hf)].astype(f32)
                + ring[1][m][...].astype(f32)
                + ring[2][m][...].astype(f32)
            ).astype(bf16)
            if u == 4:
                g1_out[0, pl.ds(m * hf, hf), :] = total
            elif u % 2 == 0:
                g2_out[1 - i, pl.ds(m * hf, hf), :] = total
            else:
                part_z[i, m] = total
        if u % 2:
            last_copy(u).start()

    def close(u):
        i = u // 2
        last_copy(u).wait_recv()
        g1_out[1 - i] = (part_z[i, h].astype(f32) + got_z[i].astype(f32)).astype(bf16)

    def give(i):
        for n in range(NC):
            send_back(back[i][n])

    def arrive(*copies):
        for m in copies:
            z_copies[m].wait_recv()

    def exchange(first_copy, end):
        for m in range(first_copy, end):
            z_copies[m].start()

    @pl.when(p < 2)
    def _():
        early.start()

    def run(order):
        for task in order:
            if callable(task[0]):
                task[0](*task[1:])
            else:
                @pl.when(jnp.logical_and(p >= task[0], p <= task[1]))
                def _():
                    if len(task) == 2:
                        settle(task[0] == 7, task[0] > 0)
                    else:
                        task[2](*task[3:])

    @pl.when(p > 5)
    def _():
        run([
            (6, 6, exchange, 1, 2),
            (7, 7),
            (7, 7, exchange, 1, 2),
            (product, 1), (pair_sum, 1),
            (6, 6),
            (arrive, 0, 1), (6, 6, exchange, 2, 3), (exchange, 3, 4),
            (product, 0), (pair_sum, 0),
            (arrive, 2, 3), (exchange, 4, 6),
            (product, 2), (pass_on, 1), (pair_sum, 2), (pass_on, 0), (finish, 1), (give, 0), (give, 1),
            (arrive, 4, 5), (product, 4), (pass_on, 2), (pair_sum, 4), (finish, 0), (close, 1), (pass_on, 4),
            (finish, 2), (finish, 4),
        ])
        core_copy(4).wait_send()
        for copy in ring_copies(4):
            copy.wait_send()
        for copy in z_copies[4:]:
            copy.wait_send()

    @pl.when(p < 6)
    def _():
        run([
            (product, 1), (product, 3), (pair_sum, 1), (exchange, 1, 2), (pair_sum, 3),
            (arrive, 0, 1), (exchange, 2, 4), (product, 0), (give, 0), (pass_on, 1), (pair_sum, 0),
            (5, 5),
            (arrive, 2, 3), (product, 2), (pass_on, 3), (pair_sum, 2),
            (4, 4),
            (finish, 1), (pass_on, 0),
            (3, 3),
            (finish, 3), (pass_on, 2), (close, 1), (finish, 0), (close, 3), (finish, 2),
            (1, 2), (0, 0),
        ])
        core_copy(3).wait_send()
        for copy in ring_copies(3):
            copy.wait_send()
        last_copy(3).wait_send()

    for copy in z_copies[:4]:
        copy.wait_send()
    for u in range(3):
        core_copy(u).wait_send()
        for copy in ring_copies(u):
            copy.wait_send()
    last_copy(1).wait_send()

    @pl.when(p < 7)
    def _():
        for pair in v_send:
            for copy in pair:
                copy.wait_send()

    @pl.when(p > 0)
    def _():
        for pair in a_send:
            for copy in pair:
                copy.wait_send()

    @pl.when(p < 6)
    def _():
        give(1)

    for m in range(2):
        @pl.when(away[m])
        def _():
            for i in range(2):
                swap[2 * i + m].wait_send()
            for i, (home, out) in enumerate(((home_s, ns_out), (home_a, na_out))):
                for k in range(NC):
                    back[i][k][m].wait()
                    out[0, halves[m], cs(k)] = home[k, halves[m], :]


def leave(*refs):
    for i in range(4):
        refs[4 + i][...] = refs[i][...]


def body(coarse_guess, adjoint_guess, w_first, w_second):
    layers, width, hidden = w_first.shape
    rows = coarse_guess.shape[1]
    col = width // NC
    vmem = pltpu.VMEM
    dma = pltpu.SemaphoreType.DMA
    hw, sw = hidden // 16, width // 16
    shapes = (
        jax.ShapeDtypeStruct((1, rows, width), bf16),
        jax.ShapeDtypeStruct((1, rows, width), bf16),
        jax.ShapeDtypeStruct((layers, sw, hidden), bf16),
        jax.ShapeDtypeStruct((layers, hw, width), bf16),
    )
    held = pl.pallas_call(
        kernel,
        out_shape=shapes,
        in_specs=[pl.BlockSpec(memory_space=pl.ANY)] * 4,
        out_specs=[pl.BlockSpec(memory_space=pltpu.VMEM)] * 4,
        scratch_shapes=[
            vmem((layers, width, hidden), bf16),
            vmem((layers, hidden, width), bf16),
            vmem((hidden, width), bf16),
            vmem((width, hidden), bf16),
            vmem((rows, width), bf16),
            vmem((rows, width), bf16),
            vmem((NC, rows, col), bf16),
            vmem((NC, rows, col), bf16),
            vmem((NC, rows, col), bf16),
            vmem((NC, rows, col), bf16),
            vmem((rows, hidden), f32),
            vmem((rows, hidden), f32),
            vmem((rows, width), f32),
            vmem((rows, width), f32),
            vmem((rows, width), f32),
            vmem((2, rows, hidden // 2), bf16),
            vmem((2, rows, hidden // 2), bf16),
            vmem((rows, width), bf16),
            vmem((NC, rows, col), bf16),
            vmem((2, 2 * rows, hidden // 2), bf16),
            vmem((2, 2 * rows, width), bf16),
            vmem((2, 2 * rows, col), bf16),
            vmem((2 * rows, hidden), bf16),
            vmem((2, rows, hidden), bf16),
            vmem((rows, hidden), bf16),
            vmem((rows, hidden), f32),
            vmem((hidden, width), bf16),
            vmem((NC, rows, col), bf16),
            vmem((NC, rows, col), bf16),
            vmem((2, 2, sw, hidden), bf16),
            vmem((2, sw, hidden), bf16),
            vmem((2, 4 * hw, width), bf16),
            vmem((2, 8 * sw, hidden), bf16),
            vmem((2, 3, 2, hw // 2, width), bf16),
            vmem((2, 3, 2, sw, hidden), bf16),
            dma((12,)),
            dma((2 * NC,)),
            dma((2 * NC,)),
            dma((2 * NC,)),
            dma((2 * NC,)),
            dma((6,)),
            dma((6,)),
            dma((4,)),
            dma((4,)),
            dma((24,)),
            dma((24,)),
            dma((4 + 4 * NC,)),
            dma((4 + 4 * NC,)),
            dma((2,)),
            dma((2,)),
        ],
        compiler_params=pltpu.CompilerParams(
            collective_id=0, has_side_effects=True, vmem_limit_bytes=60 << 20
        ),
        name="mgrit",
    )(coarse_guess, adjoint_guess, w_first, w_second)
    return pl.pallas_call(
        leave,
        out_shape=shapes,
        in_specs=[pl.BlockSpec(memory_space=pltpu.VMEM)] * 4,
        out_specs=[pl.BlockSpec(memory_space=pltpu.VMEM)] * 4,
        name="leave",
    )(*held)


def solution(mesh):
    in_specs = (
        P("layer", "dp", None),
        P("layer", "dp", None),
        P("layer", None, None),
        P("layer", None, None),
    )
    out_specs = (
        P("layer", "dp", None),
        P("layer", "dp", None),
        P("layer", "dp", None),
        P("layer", "dp", None),
    )
    return jax.shard_map(body, mesh=mesh, in_specs=in_specs, out_specs=out_specs, check_vma=False)
```

```python
import functools

import jax
import jax.numpy as jnp
from jax import lax
from jax.experimental import pallas as pl
from jax.experimental.pallas import tpu as pltpu
from jax.sharding import PartitionSpec as P

MESH = pl.DeviceIdType.MESH
f32 = jnp.float32
bf16 = jnp.bfloat16
STEP = 0.25
NC = 4
NT = (((1,), (1,)), ((), ()))
TN = (((0,), (0,)), ((), ()))


def mm(x, w):
    return jnp.dot(x, w, preferred_element_type=f32)


def mm_nt(x, w):
    return lax.dot_general(x, w, NT, preferred_element_type=f32)


def mm_tn(x, w):
    return lax.dot_general(x, w, TN, preferred_element_type=f32)


def slope_of(pre):
    sig = jax.nn.sigmoid(pre)
    return sig * (1.0 + pre * (1.0 - sig))


def kernel(
    g_hbm, a_hbm, w1_hbm, w2_hbm,
    ns_out, na_out, g1_out, g2_out,
    w1, w2, w1t, w2t, g, a,
    vbuf, nbuf, arr, abuf, pre0, work, base, out0, y1,
    act0, act1, s1p, s1c,
    lhs_a, rhs_y, dpre, dl, acc, w1t1, home_s, home_a, part_z, got_z,
    core_a, core_s, ring_a, ring_s,
    ld, vs, vr, asn, ar, zs, zr, ds, dr, ys, yr, hs_s, hs_r, fs, fr,
):
    rows, width = g.shape
    hidden = w1.shape[2]
    col = width // NC
    half = hidden // 2
    hid = hidden // 4
    p = lax.axis_index("layer")
    dp = lax.axis_index("dp")
    h = dp // 8
    y = (dp // 2) % 4
    c = dp % 2
    y_up, y_dn, y_far = (y + 1) % 4, (y + 3) % 4, (y + 2) % 4
    at_z = (p, (1 - h) * 8 + y * 2 + c)
    at_core = (p, h * 8 + y * 2 + (1 - c))
    at_up = (p, h * 8 + y_up * 2 + c)
    at_dn = (p, h * 8 + y_dn * 2 + c)
    other = (1 - h) * 8 + y * 2 + c
    zhop = 1 - p % 2
    at_next, at_prev = (), ()
    for m in range(2):
        turn_next = zhop * m + (1 - zhop) * c
        turn_prev = (1 - zhop) * m + zhop * c
        at_next += (((p + 1) % 8, dp * (1 - turn_next) + other * turn_next),)
        at_prev += (((p + 7) % 8, dp * (1 - turn_prev) + other * turn_prev),)
    away = [(m * ((p + 1) // 2) + c * (p // 2)) % 2 == 1 for m in range(2)]
    rh = rows // 2
    halves = (pl.ds(0, rh), pl.ds(rh, rh))

    barrier = pltpu.get_barrier_semaphore()
    for peer in (at_z, at_core, at_up, at_dn, *at_next, *at_prev):
        pl.semaphore_signal(barrier, inc=1, device_id=peer, device_id_type=MESH)

    loads = []
    for layer in range(2):
        for store, src in ((w1, w1_hbm), (w2, w2_hbm)):
            size = store.shape[2] // 2
            for m in range(2):
                at = (layer, slice(None), pl.ds(m * size, size))
                loads.append(pltpu.make_async_copy(src.at[at], store.at[at], ld.at[len(loads)]))
    local = [
        pltpu.make_async_copy(src.at[0, halves[m]], dst.at[halves[m]], ld.at[8 + 2 * i + m])
        for i, (src, dst) in enumerate(((g_hbm, g), (a_hbm, a)))
        for m in range(2)
    ]

    def guess(what, i, remote_copies):
        for m in range(2):
            @pl.when(away[m])
            def _():
                if what == "remote":
                    remote_copies[2 * i + m].start()
                elif what == "wait":
                    remote_copies[2 * i + m].wait_recv()

            @pl.when(jnp.logical_not(away[m]))
            def _():
                if what == "local":
                    local[2 * i + m].start()
                elif what == "wait":
                    local[2 * i + m].wait()

    def remote(src, dst, ss, rs, dev):
        return pltpu.make_async_remote_copy(
            src_ref=src, dst_ref=dst, send_sem=ss, recv_sem=rs, device_id=dev, device_id_type=MESH
        )

    def hop(src, dst, ss, rs, peers):
        return [
            [
                remote(src.at[k, at], dst.at[k, at], ss.at[2 * k + m], rs.at[2 * k + m], peers[m])
                for m, at in enumerate(halves)
            ]
            for k in range(NC)
        ]

    v_send = hop(nbuf, vbuf, vs, vr, at_next)
    a_send = hop(abuf, arr, asn, ar, at_prev)
    swap = [
        remote(src.at[0, halves[m]], dst.at[halves[m]], hs_s.at[2 * i + m], hs_r.at[2 * i + m], at_z)
        for i, (src, dst) in enumerate(((g_hbm, g), (a_hbm, a)))
        for m in range(2)
    ]
    back = [
        [
            [
                remote(
                    src.at[k, halves[m]], dst.at[k, halves[m]],
                    hs_s.at[4 + (i * NC + k) * 2 + m], hs_r.at[4 + (i * NC + k) * 2 + m], at_z,
                )
                for m in range(2)
            ]
            for k in range(NC)
        ]
        for i, (src, dst) in enumerate(((nbuf, home_s), (abuf, home_a)))
    ]

    def send_back(copies):
        for m in range(2):
            @pl.when(away[m])
            def _():
                copies[m].start()

    def hs(j):
        return pl.ds(j * hid, hid)

    def cs(n):
        return pl.ds(n * col, col)

    def second(act, layer, n):
        return mm(act[0], w2[layer, pl.ds(0, half), cs(n)]) + mm(
            act[1], w2[layer, pl.ds(half, half), cs(n)]
        )

    def put_act(act, j, value):
        act[j // 2, :, pl.ds((j % 2) * hid, hid)] = value

    guess("local", 0, swap)
    for load in loads:
        load.start()
    guess("local", 1, swap)

    @pl.when(p > 0)
    def _():
        pl.semaphore_wait(barrier, 8)

    guess("remote", 0, swap)
    guess("remote", 1, swap)
    guess("wait", 0, swap)
    for j in range(4):
        if j % 2 == 0:
            loads[j // 2].wait()
        pre = mm(g[...], w1[0, :, hs(j)])
        pre0[:, hs(j)] = pre
        put_act(act0, j, (pre * jax.nn.sigmoid(pre)).astype(bf16))
    for n in range(NC):
        if n % 2 == 0:
            loads[2 + n // 2].wait()
        out = second(act0, 0, n)
        out0[:, cs(n)] = out
        s1p[:, cs(n)] = (g[:, cs(n)].astype(f32) + STEP * out).astype(bf16)
    for j in range(4):
        if j % 2 == 0:
            loads[4 + j // 2].wait()
        pre = mm(s1p[...], w1[1, :, hs(j)])
        put_act(act1, j, (pre * jax.nn.sigmoid(pre)).astype(bf16))

    @pl.when(p == 0)
    def _():
        pl.semaphore_wait(barrier, 8)

    for n in range(NC):
        if n % 2 == 0:
            loads[6 + n // 2].wait()
        begin = g[:, cs(n)].astype(f32)
        out = out0[:, cs(n)]
        relaxed = begin + STEP * out + STEP * second(act1, 1, n)
        base_n = relaxed - (begin + 2 * STEP * out)
        base[:, cs(n)] = base_n

        @pl.when(p == 0)
        def _():
            vbuf[n] = g[:, cs(n)]
            nbuf[n] = (base_n + (begin + 2 * STEP * out)).astype(bf16)
            for copy in v_send[n]:
                copy.start()

    guess("wait", 1, swap)
    early = remote(a, rhs_y.at[0, pl.ds(rows, rows)], zs.at[0], zr.at[0], at_z)

    @pl.when(p > 1)
    def _():
        early.start()

    def prepare():
        for j in range(4):
            work[:, hs(j)] = STEP * mm_nt(a[...], w2[1, hs(j), :])

    def transpose():
        for j in range(4):
            for n in range(NC):
                w2t[cs(n), hs(j)] = w2[0, hs(j), cs(n)].T
                w1t[hs(j), cs(n)] = w1[0, cs(n), hs(j)].T
                w1t1[hs(j), cs(n)] = w1[1, cs(n), hs(j)].T

    @pl.when(p > 0)
    def _():
        prepare()

    def pull(k, save=True):
        diff = (arr[k].astype(f32) - a[:, cs(k)].astype(f32)).astype(bf16)
        for j in range(4):
            pulled = mm(diff, w2t[cs(k), hs(j)])
            if k:
                pulled = pulled + acc[:, hs(j)]
            if save:
                acc[:, hs(j)] = pulled
            else:
                dl[:, hs(j)] = (2 * STEP * pulled * pre0[:, hs(j)]).astype(bf16)

    @pl.when(p > 1)
    def _():
        transpose()

    @pl.when(p == 7)
    def _():
        for k in range(NC):
            arr[k] = a[:, cs(k)]
        for k in range(NC):
            pull(k)

    @pl.when(p > 0)
    def _():
        for k in range(NC):
            for copy in v_send[k]:
                copy.wait_recv()
            for j in range(4):
                pre = mm(vbuf[k], w1[0, cs(k), hs(j)])
                if k:
                    pre = pre + pre0[:, hs(j)]
                pre0[:, hs(j)] = pre
                if k == NC - 1:
                    put_act(act0, j, (pre * jax.nn.sigmoid(pre)).astype(bf16))

    def advance(sending):
        for n in range(NC):
            out = second(act0, 0, n)
            out0[:, cs(n)] = out
            new = (base[:, cs(n)] + (vbuf[n].astype(f32) + 2 * STEP * out)).astype(bf16)
            nbuf[n] = new
            if sending:
                for copy in v_send[n]:
                    copy.start()

    @pl.when(jnp.logical_and(p > 0, p < 7))
    def _():
        advance(True)

    @pl.when(p == 7)
    def _():
        advance(False)

    @pl.when(p == 0)
    def _():
        prepare()

    @pl.when(p < 2)
    def _():
        transpose()

    def part(u):
        i = u // 2
        size, start = 128, 0
        if u % 2 == 0:
            start = i * 8 * size
            store, got = w2.at[1], core_a.at[i]
            ring = [[ring_a.at[i, n, m] for m in range(2)] for n in range(3)]
        else:
            store, got = w1.at[1 - i], core_s.at[i]
            ring = [[ring_s.at[i, n, m] for m in range(2)] for n in range(3)]

        def block(cc, yy, lo=0, n=size):
            return pl.ds(pl.multiple_of(start + (cc * 4 + yy) * size + lo, size // 2), n)

        return size, store, block, got, ring

    def core_copy(u):
        size, store, block, got, ring = part(u)
        return remote(store.at[block(1 - c, 0, 0, 4 * size)], got, ds.at[u], dr.at[u], at_core)

    def ring_copies(u):
        size, store, block, got, ring = part(u)
        hf = size // 2
        plan = [
            (block(c, y_far, 0, hf), (0, 0), at_up),
            (block(c, y_far, hf, hf), (0, 1), at_dn),
            (block(c, y_up, hf, hf), (1, 1), at_up),
            (block(c, y_dn, 0, hf), (2, 0), at_dn),
            (block(c, y_up, 0, hf), (1, 0), at_up),
            (block(c, y_dn, hf, hf), (2, 1), at_dn),
        ]
        return [
            remote(store.at[src], ring[dst[0]][dst[1]], ys.at[u * 6 + m], yr.at[u * 6 + m], dev)
            for m, (src, dst, dev) in enumerate(plan)
        ]

    def last_copy(u):
        i = u // 2
        return remote(part_z.at[i, 1 - h], got_z.at[i], fs.at[i], fr.at[i], at_z)

    def product(u):
        size, store, block, got, ring = part(u)
        i = u // 2
        if u % 2 == 0:
            if i == 0:
                rhs_y[0, pl.ds(0, rows), :] = a[...]
            lhs_a[i, pl.ds(0, rows), :] = (act1 if i == 0 else act0)[h]
            for yy in range(4):
                res = STEP * mm_tn(lhs_a[i, :, pl.ds(yy * 2 * size, 2 * size)], rhs_y[i])
                res = res.astype(bf16)
                for cc in range(2):
                    store[block(cc, yy)] = res[cc * size:(cc + 1) * size]
        else:
            hf = size // 2
            for kk in range(4):
                lhs = (s1c if i == 0 else vbuf)[kk]
                for piece in range(2):
                    at = pl.ds(piece * half, half)
                    res = mm_tn(lhs, dpre[i, :, at]).astype(bf16)
                    for m in range(4):
                        rows_at = block(m % 2, (kk % 2) * 2 + m // 2, (kk // 2) * hf, hf)
                        store[rows_at, at] = res[m * hf:(m + 1) * hf]
        core_copy(u).start()

    def pair_sum(u):
        size, store, block, got, ring = part(u)
        core_copy(u).wait_recv()
        copies = ring_copies(u)

        def add(yy):
            at = pl.ds(pl.multiple_of(yy * size, size), size)
            store[block(c, yy)] = (store[block(c, yy)].astype(f32) + got[at].astype(f32)).astype(bf16)

        add(y_far)
        copies[0].start()
        copies[1].start()
        add(y_up)
        copies[2].start()
        add(y_dn)
        copies[3].start()
        add(y)

    def pass_on(u):
        size, store, block, got, ring = part(u)
        hf = size // 2
        copies = ring_copies(u)
        for m, yy, lo in ((0, y_up, 0), (1, y_dn, hf)):
            copies[m].wait_recv()
            at = block(c, yy, lo, hf)
            store[at] = (store[at].astype(f32) + ring[0][m][...].astype(f32)).astype(bf16)
            copies[4 + m].start()

    def finish(u):
        size, store, block, got, ring = part(u)
        hf = size // 2
        i = u // 2
        copies = ring_copies(u)
        for m in (2, 3, 4, 5):
            copies[m].wait_recv()
        for m in range(2):
            total = (
                store[block(c, y, m * hf, hf)].astype(f32)
                + ring[1][m][...].astype(f32)
                + ring[2][m][...].astype(f32)
            ).astype(bf16)
            if u % 2 == 0:
                g2_out[1 - i, pl.ds(m * hf, hf), :] = total
            else:
                part_z[i, m] = total
        if u % 2:
            last_copy(u).start()

    def close(u):
        i = u // 2
        last_copy(u).wait_recv()
        g1_out[1 - i] = (part_z[i, h].astype(f32) + got_z[i].astype(f32)).astype(bf16)

    for n in range(NC):
        ns_out[0, :, cs(n)] = nbuf[n]

    z_copies = [
        early,
        remote(act1.at[1 - h], lhs_a.at[0, pl.ds(rows, rows)], zs.at[1], zr.at[1], at_z),
        remote(act0.at[1 - h], lhs_a.at[1, pl.ds(rows, rows)], zs.at[2], zr.at[2], at_z),
        remote(rhs_y.at[1, pl.ds(0, rows)], rhs_y.at[1, pl.ds(rows, rows)], zs.at[3], zr.at[3], at_z),
    ]
    @pl.when(p == 7)
    def _():
        z_copies[2].start()

    for n in range(NC):
        state = (vbuf[n].astype(f32) + STEP * out0[:, cs(n)]).astype(bf16)
        s1p[:, cs(n)] = state
        s1c[n] = state
    for j in range(4):
        pre = mm(s1p[...], w1[1, :, hs(j)])
        sig = jax.nn.sigmoid(pre)
        put_act(act1, j, (pre * sig).astype(bf16))
        dpre[0, :, hs(j)] = (
            work[:, hs(j)] * (sig * (1.0 + pre * (1.0 - sig)))
        ).astype(bf16)
        pre0[:, hs(j)] = slope_of(pre0[:, hs(j)])

    product(1)

    for n in range(NC):
        y1_n = a[:, cs(n)].astype(f32) + mm(dpre[0], w1t1[:, cs(n)])
        y1[:, cs(n)] = y1_n
        rhs_y[1, pl.ds(0, rows), cs(n)] = y1_n.astype(bf16)
    for j in range(4):
        pulled = STEP * mm(rhs_y[1, pl.ds(0, rows), :], w2t[:, hs(j)])
        dpre[1, :, hs(j)] = (pulled * pre0[:, hs(j)]).astype(bf16)
    for n in range(NC):
        y1[:, cs(n)] = y1[:, cs(n)] + mm(dpre[1], w1t[:, cs(n)])

    def settle(end, sending=True):
        if end:
            for j in range(4):
                dl[:, hs(j)] = (2 * STEP * acc[:, hs(j)] * pre0[:, hs(j)]).astype(bf16)
        else:
            for k in range(NC):
                for copy in a_send[k]:
                    copy.wait_recv()
                pull(k, k < NC - 1)
        for n in range(NC):
            lifted = mm(dl[...], w1t[:, cs(n)])
            diff = arr[n].astype(f32) - a[:, cs(n)].astype(f32)
            abuf[n] = (y1[:, cs(n)] + diff + lifted).astype(bf16)
            if sending:
                for copy in a_send[n]:
                    copy.start()
        for n in range(NC):
            na_out[0, :, cs(n)] = abuf[n]

    def give(i):
        for n in range(NC):
            send_back(back[i][n])

    def arrive(*copies):
        for m in copies:
            z_copies[m].wait_recv()

    def exchange(first_copy, end):
        for m in range(first_copy, end):
            z_copies[m].start()

    @pl.when(p < 2)
    def _():
        early.start()

    def run(order):
        for task in order:
            if callable(task[0]):
                task[0](*task[1:])
            else:
                @pl.when(jnp.logical_and(p >= task[0], p <= task[1]))
                def _():
                    if len(task) == 2:
                        settle(task[0] == 7, task[0] > 0)
                    else:
                        task[2](*task[3:])

    run([
        (7, 7), (7, 7, exchange, 1, 2), (7, 7, exchange, 3, 4),
        (product, 3), (pair_sum, 1), (0, 5, exchange, 1, 4),
        (6, 6), (6, 6, exchange, 1, 4),
        (pair_sum, 3), (arrive, 0, 1), (product, 0), (pass_on, 1), (arrive, 2, 3), (product, 2), (pair_sum, 0), (give, 0),
        (5, 5),
        (pass_on, 3), (pair_sum, 2),
        (4, 4),
        (finish, 1), (pass_on, 0),
        (3, 3),
        (finish, 3), (pass_on, 2), (close, 1), (6, 7, give, 1),
        (finish, 0), (close, 3), (finish, 2),
        (1, 2), (0, 0),
    ])
    for copy in z_copies:
        copy.wait_send()
    for u in range(4):
        core_copy(u).wait_send()
        for copy in ring_copies(u):
            copy.wait_send()
    for u in (1, 3):
        last_copy(u).wait_send()

    @pl.when(p < 7)
    def _():
        for pair in v_send:
            for copy in pair:
                copy.wait_send()

    @pl.when(p > 0)
    def _():
        for pair in a_send:
            for copy in pair:
                copy.wait_send()

    @pl.when(p < 6)
    def _():
        give(1)

    for m in range(2):
        @pl.when(away[m])
        def _():
            for i in range(2):
                swap[2 * i + m].wait_send()
            for i, (home, out) in enumerate(((home_s, ns_out), (home_a, na_out))):
                for k in range(NC):
                    back[i][k][m].wait()
                    out[0, halves[m], cs(k)] = home[k, halves[m], :]


def leave(*refs):
    for i in range(4):
        refs[4 + i][...] = refs[i][...]


def body(coarse_guess, adjoint_guess, w_first, w_second):
    layers, width, hidden = w_first.shape
    rows = coarse_guess.shape[1]
    col = width // NC
    vmem = pltpu.VMEM
    dma = pltpu.SemaphoreType.DMA
    hw, sw = hidden // 16, width // 16
    shapes = (
        jax.ShapeDtypeStruct((1, rows, width), bf16),
        jax.ShapeDtypeStruct((1, rows, width), bf16),
        jax.ShapeDtypeStruct((layers, sw, hidden), bf16),
        jax.ShapeDtypeStruct((layers, hw, width), bf16),
    )
    held = pl.pallas_call(
        kernel,
        out_shape=shapes,
        in_specs=[pl.BlockSpec(memory_space=pl.ANY)] * 4,
        out_specs=[pl.BlockSpec(memory_space=pltpu.VMEM)] * 4,
        scratch_shapes=[
            vmem((layers, width, hidden), bf16),
            vmem((layers, hidden, width), bf16),
            vmem((hidden, width), bf16),
            vmem((width, hidden), bf16),
            vmem((rows, width), bf16),
            vmem((rows, width), bf16),
            vmem((NC, rows, col), bf16),
            vmem((NC, rows, col), bf16),
            vmem((NC, rows, col), bf16),
            vmem((NC, rows, col), bf16),
            vmem((rows, hidden), f32),
            vmem((rows, hidden), f32),
            vmem((rows, width), f32),
            vmem((rows, width), f32),
            vmem((rows, width), f32),
            vmem((2, rows, hidden // 2), bf16),
            vmem((2, rows, hidden // 2), bf16),
            vmem((rows, width), bf16),
            vmem((NC, rows, col), bf16),
            vmem((2, 2 * rows, hidden // 2), bf16),
            vmem((2, 2 * rows, width), bf16),
            vmem((2, rows, hidden), bf16),
            vmem((rows, hidden), bf16),
            vmem((rows, hidden), f32),
            vmem((hidden, width), bf16),
            vmem((NC, rows, col), bf16),
            vmem((NC, rows, col), bf16),
            vmem((2, 2, sw, hidden), bf16),
            vmem((2, sw, hidden), bf16),
            vmem((2, 4 * hw, width), bf16),
            vmem((2, 8 * sw, hidden), bf16),
            vmem((2, 3, 2, hw // 2, width), bf16),
            vmem((2, 3, 2, sw, hidden), bf16),
            dma((12,)),
            dma((2 * NC,)),
            dma((2 * NC,)),
            dma((2 * NC,)),
            dma((2 * NC,)),
            dma((4,)),
            dma((4,)),
            dma((4,)),
            dma((4,)),
            dma((24,)),
            dma((24,)),
            dma((4 + 4 * NC,)),
            dma((4 + 4 * NC,)),
            dma((2,)),
            dma((2,)),
        ],
        compiler_params=pltpu.CompilerParams(
            collective_id=0, has_side_effects=True, vmem_limit_bytes=60 << 20
        ),
        name="mgrit",
    )(coarse_guess, adjoint_guess, w_first, w_second)
    return pl.pallas_call(
        leave,
        out_shape=shapes,
        in_specs=[pl.BlockSpec(memory_space=pltpu.VMEM)] * 4,
        out_specs=[pl.BlockSpec(memory_space=pltpu.VMEM)] * 4,
        name="leave",
    )(*held)


def solution(mesh):
    in_specs = (
        P("layer", "dp", None),
        P("layer", "dp", None),
        P("layer", None, None),
        P("layer", None, None),
    )
    out_specs = (
        P("layer", "dp", None),
        P("layer", "dp", None),
        P("layer", "dp", None),
        P("layer", "dp", None),
    )
    return jax.shard_map(body, mesh=mesh, in_specs=in_specs, out_specs=out_specs, check_vma=False)
```
